512 devices in a mesh: seq: 64 (over y, z), chan: 8 (over x, core).
Axes of the slice: x: 4, y: 8, z: 8, core: 2. Of those that a mesh axis runs over, the one named last changes fastest.
Arguments:
- tokens: bfloat16 [16384, 8192], P('seq', 'chan'), may hold values from -6 to 6
- in_weight: bfloat16 [8192, 3, 2048], P('seq', None, 'chan')
- rate: float32 [2048, 16], P('chan'), as said below
- residue: float32 [2048, 16], P('chan')
- skip_gain: float32 [2048], P('chan'), may hold values from 0.5 to 1.5
Outputs:
- mixed: bfloat16 [16384, 2048], P('seq', 'chan')
- state_unit: float32 [2048, 16], P(('chan', 'seq'))
- state_scale: float32 [2048], P(('chan', 'seq'))
The draws below stay inside these ranges and needn't reach their ends.
Inputs may be any that keep to these rules, and one draw needn't show every extreme that they name: rate is positive and below 1/25.
All inputs are finite; a program needn't handle non-finite values. Where the reference program divides by a largest or mean magnitude, that divisor is 1e-20 or more.
Results may differ from the reference program's by a relative error of at most 0.0096.
Values may be sent and summed in bfloat16 or wider, within the bound.
No kernel may reach another device: no remote copies, remote signals or barrier semaphores. Data moves between devices by JAX's collectives and lax.ppermute only.
A program may use at most 64 MiB of HBM per device.

```python
import jax
import jax.numpy as jnp

D = 8192
CHANNELS = 2048
POLES = 16
TOKENS = 16384


def pole_rates(key, fast_share):
    pick = jax.random.uniform(jax.random.fold_in(key, 11), (CHANNELS, POLES))
    fast = jnp.exp(jax.random.uniform(jax.random.fold_in(key, 12), (CHANNELS, POLES), minval=jnp.log(1.0 / 50.0), maxval=jnp.log(1.0 / 30.0)))
    slow = jnp.exp(jax.random.uniform(jax.random.fold_in(key, 13), (CHANNELS, POLES), minval=jnp.log(0.05 / TOKENS), maxval=jnp.log(1.0 / TOKENS)))
    return jnp.where(pick < fast_share, fast, slow).astype(jnp.float32)


def draw_in_weight(key, part):
    key = jax.random.fold_in(key, 7)
    values = jnp.clip(jax.random.normal(jax.random.fold_in(key, 1), (D, 3, CHANNELS)), -6.0, 6.0)
    pick = jax.random.uniform(jax.random.fold_in(key, 2), (CHANNELS,))
    quiet = jnp.exp(jax.random.uniform(jax.random.fold_in(key, 3), (CHANNELS,), minval=jnp.log(0.0003), maxval=jnp.log(0.0015)))
    factor = jnp.where(pick < 0.125, quiet, 1.0)
    ones_row = jnp.ones((CHANNELS,), jnp.float32)
    stream_scale = jnp.stack([ones_row, ones_row, factor], axis=0)
    return (values * stream_scale[None] * 0.6 / jnp.sqrt(jnp.float32(D))).astype(jnp.bfloat16)


def draw_rate(key, part):
    share = 0.5
    rates = pole_rates(key, share)
    return rates


def draw_residue(key, part):
    share = 0.5
    rates = pole_rates(key, share)
    key = jax.random.fold_in(key, 5)
    values = jax.random.normal(key, (CHANNELS, POLES))
    return (values * jnp.sqrt(2.0 * rates) * 0.25).astype(jnp.float32)


def levels(rng, extent, cuts, smallest, high):
    def one(position, shards_of):
        steps = jax.random.uniform(jax.random.fold_in(jax.random.fold_in(rng, 6), position), (shards_of,), jnp.float32, smallest / len(cuts), high / len(cuts))
        return jnp.repeat(jnp.exp(steps), extent[position] // shards_of).reshape((-1,) + (1,) * (len(extent) - position - 1))

    gain = one(*cuts[0])
    for cut in cuts[1:]:
        gain = gain * one(*cut)
    return gain


def gaussian(rng, shape, spread, bound, shards=(), kind=jnp.bfloat16):
    factor_of = levels(rng, shape, shards, -0.22, 0.18) if shards else 1.0
    array = jax.random.normal(rng, shape, jnp.float32) * spread * factor_of
    return jnp.minimum(jnp.maximum(array, -bound), bound).astype(kind)


def setup_inputs(seed: int = 0) -> dict:
    seeds = jax.random.split(jax.random.key(seed), 6)
    tokens = gaussian(seeds[0], (TOKENS, D), 1.0, 6.0, ((0, 64), (1, 8)))
    in_weight = draw_in_weight(jax.random.fold_in(seeds[5], 71), 0)
    rate = draw_rate(jax.random.fold_in(seeds[5], 71), 0)
    residue = draw_residue(jax.random.fold_in(seeds[5], 71), 0)
    skip_gain = jnp.clip(0.5 + 1.0 * jax.random.uniform(seeds[4], (CHANNELS,), jnp.float32) ** levels(seeds[4], (CHANNELS,), ((0, 8),), -0.2, 0.2), 0.5, 1.5)
    return {"tokens": tokens, "in_weight": in_weight, "rate": rate, "residue": residue, "skip_gain": skip_gain}


def reference(tokens, in_weight, rate, residue, skip_gain):
    flat = in_weight.reshape(D, 3 * CHANNELS)
    projected = jnp.dot(tokens, flat, preferred_element_type=jnp.float32).astype(jnp.bfloat16)
    projected = projected.reshape(TOKENS, 3, CHANNELS)
    query = projected[:, 0].astype(jnp.float32)
    drive = projected[:, 1].astype(jnp.float32) * projected[:, 2].astype(jnp.float32)
    times = jnp.arange(TOKENS, dtype=jnp.float32)
    filt = jnp.zeros((TOKENS, CHANNELS), jnp.float32)
    state_cols = []
    for pole in range(POLES):
        decay = jnp.exp(-times[:, None] * rate[None, :, pole])
        filt = filt + residue[None, :, pole] * decay
        back = jnp.exp(-(TOKENS - 1 - times)[:, None] * rate[None, :, pole])
        state_cols.append(jnp.sum(back * drive, axis=0))
    length = 2 * TOKENS
    spectrum = jnp.fft.rfft(drive, length, axis=0) * jnp.fft.rfft(filt, length, axis=0)
    conv = jnp.fft.irfft(spectrum, length, axis=0)[:TOKENS].astype(jnp.float32)
    mixed = (query * (conv + skip_gain[None, :] * drive)).astype(jnp.bfloat16)
    state = jnp.stack(state_cols, axis=1)
    top = jnp.maximum(jnp.max(jnp.abs(state), axis=1), 1.0)
    return mixed, state / top[:, None], top / 127.0
```

```python
import functools

import jax
import jax.numpy as jnp
from jax import lax
from jax.experimental import pallas as pl
from jax.experimental.pallas import tpu as pltpu
from jax.sharding import Mesh
from jax.sharding import PartitionSpec as P

Y, Z, X, K = 8, 8, 4, 2
SUB = 8
EXACT = lax.Precision.HIGHEST


def shifted(array, axis, step):
    size = lax.axis_size(axis)
    return lax.ppermute(array, axis, [(i, (i + step) % size) for i in range(size)])


def to_all(array, axis):
    copies = jnp.broadcast_to(array[None], (lax.axis_size(axis),) + array.shape)
    return lax.all_to_all(copies, axis, 0, 0, tiled=True)


def project_kernel(order_ref, tokens_ref, weight_ref, rate_ref, query_ref, drive_ref, before_ref, own_ref, total, ends):
    step = pl.program_id(0)
    rows = tokens_ref.shape[1]
    width = query_ref.shape[1]
    poles = rate_ref.shape[0]
    depth = tokens_ref.shape[2]

    @pl.when(step == 0)
    def _():
        total[...] = jnp.zeros_like(total)

    for stream in range(3):
        block = weight_ref[:, stream].reshape(depth, width)
        total[stream] += jnp.dot(tokens_ref[0], block, preferred_element_type=jnp.float32)

    @pl.when(step == pl.num_programs(0) - 1)
    def _():
        query_ref[...] = total[0].astype(jnp.bfloat16)
        key = total[1].astype(jnp.bfloat16).astype(jnp.float32)
        value = total[2].astype(jnp.bfloat16).astype(jnp.float32)
        span = rows // SUB
        for half in range(width // 128):
            here = slice(half * 128, half * 128 + 128)
            drive_ref[half] = key[:, here] * value[:, here]
            keep = [jnp.broadcast_to(jnp.exp(-rate_ref[n : n + 1, here]), (SUB, 128)) for n in range(poles)]

            def advance(i, states):
                drive = drive_ref[half, pl.ds(i, SUB, stride=span), :]
                return [s * a + drive for s, a in zip(states, keep)]

            states = lax.fori_loop(0, span, advance, [jnp.zeros((SUB, 128), jnp.float32)] * poles, unroll=8)
            for n in range(poles):
                ends[half, n * SUB : (n + 1) * SUB, :] = states[n]
            across = jnp.exp(-rate_ref[:, here] * span)
            before = jnp.zeros((poles, 128), jnp.float32)
            for b in range(SUB):
                before_ref[half, pl.ds(b, poles, stride=SUB), :] = before
                before = before * across + ends[half, pl.ds(b, poles, stride=SUB), :]
            own_ref[:, here] = before


def finish_kernel(place_ref, query_ref, drive_ref, before_ref, rows_in_ref, far_ref, rate_ref, residue_ref, skip_ref, mixed_ref, unit_ref, scale_ref, conv):
    rows, width = query_ref.shape
    poles = rate_ref.shape[0]
    span = rows // SUB
    y, z = place_ref[0], place_ref[1]
    rate = rate_ref[...]
    plane = rate * (rows * Z)
    incoming = jnp.zeros_like(rate)
    last = jnp.zeros_like(rate)
    hop = jnp.exp(-plane)
    for other in range(Y):
        incoming = jnp.where(other < y, incoming * hop + far_ref[other], incoming)
        last = last * hop + far_ref[other]
    incoming = rows_in_ref[...] + incoming * jnp.exp(-rate * (rows * z).astype(jnp.float32))

    block = lax.broadcasted_iota(jnp.int32, (SUB, 128), 0).astype(jnp.float32) * span
    for half in range(width // 128):
        here = slice(half * 128, half * 128 + 128)
        keep = [jnp.broadcast_to(jnp.exp(-rate[n : n + 1, here]), (SUB, 128)) for n in range(poles)]
        gain = [jnp.broadcast_to(residue_ref[n : n + 1, here], (SUB, 128)) for n in range(poles)]
        skip = jnp.broadcast_to(skip_ref[:, here], (SUB, 128))
        states = [
            before_ref[half, n * SUB : (n + 1) * SUB, :] + incoming[n : n + 1, here] * jnp.exp(-rate[n : n + 1, here] * block)
            for n in range(poles)
        ]

        def advance(i, states):
            drive = drive_ref[half, pl.ds(i, SUB, stride=span), :]
            states = [s * a + drive for s, a in zip(states, keep)]
            terms = [s * g for s, g in zip(states, gain)] + [skip * drive]
            while len(terms) > 1:
                terms = [sum(terms[j : j + 2][1:], terms[j]) for j in range(0, len(terms), 2)]
            conv[half, pl.ds(i, SUB, stride=span), :] = terms[0]
            return states

        lax.fori_loop(0, span, advance, states, unroll=8)
        mixed_ref[:, here] = (query_ref[:, here].astype(jnp.float32) * conv[half]).astype(jnp.bfloat16)

    owned = (y * Z + z) * 4
    pick = lax.broadcasted_iota(jnp.int32, (8, width), 1) == lax.broadcasted_iota(jnp.int32, (8, width), 0) + owned
    pick = pick.astype(jnp.float32)
    contract = (((1,), (1,)), ((), ()))
    state = lax.dot_general(pick, last, contract, precision=EXACT, preferred_element_type=jnp.float32)
    flipped = lax.dot_general(last, pick, contract, precision=EXACT, preferred_element_type=jnp.float32)
    top = jnp.maximum(jnp.max(jnp.abs(state), axis=1, keepdims=True), 1.0)
    unit_ref[...] = (state / top)[:4]
    scale_ref[...] = (jnp.maximum(jnp.max(jnp.abs(flipped), axis=0, keepdims=True), 1.0) / 127.0)[:, :4]


def vmem():
    return pl.BlockSpec(memory_space=pltpu.VMEM)


def smem():
    return pl.BlockSpec(memory_space=pltpu.SMEM)


def shards(tokens, in_weight, rate, residue, skip_gain):
    rows, depth = tokens.shape
    width, poles = rate.shape
    y, z, x, k = (lax.axis_index(a) for a in ("y", "z", "x", "k"))

    weights = lax.all_gather(in_weight.transpose(1, 0, 2), ("y", "z"), axis=0)

    pair = jnp.stack([tokens, shifted(tokens, "k", 1)])
    ahead = shifted(pair, "x", 1)
    behind = shifted(pair, "x", -1)
    across = [shifted(pair[:1], "x", 2), shifted(pair[1:], "x", -2)]
    pieces = jnp.concatenate([pair, ahead, behind] + across)
    order = jnp.stack([2 * ((x + d) % X) + (k + e) % K for d in (0, X - 1, 1, 2) for e in (0, 1)])

    rate_rows = rate.T
    residue_rows = residue.T
    chunks = X * K
    per = weights.shape[0] // chunks
    drive_shape = (width // 128, rows, 128)
    before_shape = (width // 128, poles * SUB, 128)
    f32 = functools.partial(jax.ShapeDtypeStruct, dtype=jnp.float32)
    whole = lambda shape: pl.BlockSpec(shape, lambda i, order: (0,) * len(shape))
    query, drive, before, own = pl.pallas_call(
        project_kernel,
        grid_spec=pltpu.PrefetchScalarGridSpec(
            num_scalar_prefetch=1,
            grid=(chunks,),
            in_specs=[
                pl.BlockSpec((1, rows, depth), lambda i, order: (i, 0, 0)),
                pl.BlockSpec((per,) + weights.shape[1:], lambda i, order: (order[i], 0, 0, 0)),
                whole((poles, width)),
            ],
            out_specs=[whole((rows, width)), whole(drive_shape), whole(before_shape), whole((poles, width))],
            scratch_shapes=[pltpu.VMEM((3, rows, width), jnp.float32), pltpu.VMEM(before_shape, jnp.float32)],
        ),
        out_shape=[
            jax.ShapeDtypeStruct((rows, width), jnp.bfloat16),
            f32(drive_shape),
            f32(before_shape),
            f32((poles, width)),
        ],
        compiler_params=pltpu.CompilerParams(vmem_limit_bytes=40 * 2**20),
        name="project",
    )(order, pieces, weights, rate_rows)

    near = to_all(own, "z")
    at = jnp.arange(Z, dtype=jnp.float32)[:, None, None]
    gap = z.astype(jnp.float32) - 1.0 - at
    row_rate = rate_rows[None] * rows
    rows_in = jnp.sum(jnp.where(gap >= 0, jnp.exp(-row_rate * jnp.maximum(gap, 0.0)), 0.0) * near, axis=0)
    row_sum = jnp.sum(jnp.exp(-row_rate * (Z - 1.0 - at)) * near, axis=0)
    far = to_all(row_sum, "y")

    mixed, unit, scale = pl.pallas_call(
        finish_kernel,
        in_specs=[smem()] + [vmem()] * 8,
        out_specs=[vmem()] * 3,
        scratch_shapes=[pltpu.VMEM(drive_shape, jnp.float32)],
        out_shape=[jax.ShapeDtypeStruct((rows, width), jnp.bfloat16), f32((4, poles)), f32((1, 4))],
        compiler_params=pltpu.CompilerParams(vmem_limit_bytes=40 * 2**20),
        name="finish",
    )(jnp.stack([y, z]), query, drive, before, rows_in, far, rate_rows, residue_rows, skip_gain[None])
    return mixed, unit, scale.reshape(4)


def solution(mesh):
    fine = Mesh(mesh.devices.reshape(Y, Z, X, K), ("y", "z", "x", "k"))
    seq, chan = ("y", "z"), ("x", "k")
    in_specs = (P(seq, chan), P(seq, None, chan), P(chan, None), P(chan, None), P(chan))
    out_specs = (P(seq, chan), P(chan + seq, None), P(chan + seq))
    return jax.shard_map(shards, mesh=fine, in_specs=in_specs, out_specs=out_specs, check_vma=False)
```

```python
import functools

import jax
import jax.numpy as jnp
from jax import lax
from jax.experimental import pallas as pl
from jax.experimental.pallas import tpu as pltpu
from jax.sharding import Mesh
from jax.sharding import PartitionSpec as P

Y, Z, X, K = 8, 8, 4, 2
LINE = 8
AXES = ("y", "z", "x", "k")
SUB = 8
LANES = 128
EXACT = lax.Precision.HIGHEST


def number(y, z, x, k):
    return ((y * Z + z) * X + x) * K + k


def lines(first):
    groups = []
    for k in range(K):
        along_z = (k == 0) == first
        for x in range(X):
            for o in range(LINE):
                groups.append([number(o, i, x, k) if along_z else number(i, o, x, k) for i in range(LINE)])
    return groups


def shifted(array, axis, step):
    size = lax.axis_size(axis)
    return lax.ppermute(array, axis, [(i, (i + step) % size) for i in range(size)])


def to_all(array, axis):
    copies = jnp.broadcast_to(array[None], (lax.axis_size(axis),) + array.shape)
    return lax.all_to_all(copies, axis, 0, 0, tiled=True)


def collect_kernel(meta_ref, *refs):
    k = meta_ref[8]
    tokens_ref = refs[-1]
    place = 0
    for ref in refs[:-1]:
        for i in range(0, ref.shape[0], LINE):
            piece = meta_ref[place]
            place += 1
            for block in range(LINE):
                chunk, part = jnp.where(k == 0, piece, block), jnp.where(k == 0, block, piece)
                tokens_ref[chunk, part] = ref[i + block]


def project(features_ref, weights_ref, left, right, total, left_sems, right_sems):
    streams, _, width = total.shape
    copies = []
    for chunk in range(LINE):
        copies.append(
            (
                pltpu.make_async_copy(features_ref.at[chunk], left.at[chunk], left_sems.at[chunk]),
                pltpu.make_async_copy(weights_ref.at[chunk], right.at[chunk], right_sems.at[chunk]),
            )
        )
    for pair in copies:
        for copy in pair:
            copy.start()
    for chunk, pair in enumerate(copies):
        for copy in pair:
            copy.wait()
        rows = jnp.concatenate([left[chunk, part] for part in range(LINE)], axis=1)
        for stream in range(streams):
            block = right[chunk, :, stream].reshape(-1, width)
            product = jnp.dot(rows, block, preferred_element_type=jnp.float32)
            total[stream] = product if chunk == 0 else total[stream] + product


def drive_kernel(features_ref, weights_ref, filter_ref, local_ref, own_ref, ends, total, *scratch):
    poles, width = own_ref.shape
    halves, rows = width // LANES, total.shape[1]
    span = rows // SUB
    project(features_ref, weights_ref, *scratch[:2], total, *scratch[2:])
    key = total[0].astype(jnp.bfloat16).astype(jnp.float32)
    value = total[1].astype(jnp.bfloat16).astype(jnp.float32)
    for half in range(halves):
        here = slice(half * LANES, half * LANES + LANES)
        local_ref[half, :rows] = key[:, here] * value[:, here]
    for half in range(halves):
        here = slice(half * LANES, half * LANES + LANES)
        keep = [jnp.broadcast_to(jnp.exp(-filter_ref[n : n + 1, here]), (SUB, LANES)) for n in range(poles)]

        def advance(i, states):
            drive = local_ref[half, pl.ds(i, SUB, stride=span), :]
            return [s * a + drive for s, a in zip(states, keep)]

        states = lax.fori_loop(0, span, advance, [jnp.zeros((SUB, LANES), jnp.float32)] * poles, unroll=8)
        for n in range(poles):
            ends[half, n * SUB : (n + 1) * SUB, :] = states[n]
        across = jnp.exp(-filter_ref[:poles, here] * span)
        before = jnp.zeros((poles, LANES), jnp.float32)
        for b in range(SUB):
            local_ref[half, pl.ds(rows + b, poles, stride=SUB), :] = before
            before = before * across + ends[half, pl.ds(b, poles, stride=SUB), :]
        own_ref[:, here] = before


def convolve_kernel(meta_ref, local_ref, rows_in_ref, far_ref, filter_ref, conv_ref, unit_ref, scale_ref):
    halves, rows, _ = conv_ref.shape
    poles, width = rows_in_ref.shape
    span = rows // SUB
    y, z = meta_ref[9], meta_ref[10]
    rate = filter_ref[:poles]
    incoming = jnp.zeros_like(rate)
    last = jnp.zeros_like(rate)
    hop = jnp.exp(-rate * (rows * Z))
    for other in range(Y):
        incoming = jnp.where(other < y, incoming * hop + far_ref[other], incoming)
        last = last * hop + far_ref[other]
    incoming = rows_in_ref[...] + incoming * jnp.exp(-rate * (rows * z).astype(jnp.float32))

    block = lax.broadcasted_iota(jnp.int32, (SUB, LANES), 0).astype(jnp.float32) * span
    for half in range(halves):
        here = slice(half * LANES, half * LANES + LANES)
        keep = [jnp.broadcast_to(jnp.exp(-rate[n : n + 1, here]), (SUB, LANES)) for n in range(poles)]
        gain = [jnp.broadcast_to(filter_ref[poles + n : poles + n + 1, here], (SUB, LANES)) for n in range(poles)]
        skip = jnp.broadcast_to(filter_ref[2 * poles : 2 * poles + 1, here], (SUB, LANES))
        states = [
            local_ref[half, rows + n * SUB : rows + (n + 1) * SUB, :] + incoming[n : n + 1, here] * jnp.exp(-rate[n : n + 1, here] * block)
            for n in range(poles)
        ]

        def advance(i, states):
            drive = local_ref[half, pl.ds(i, SUB, stride=span), :]
            states = [s * a + drive for s, a in zip(states, keep)]
            terms = [s * g for s, g in zip(states, gain)]
            while len(terms) > 1:
                terms = [a + b for a, b in zip(terms[::2], terms[1::2])]
            conv_ref[half, pl.ds(i, SUB, stride=span), :] = terms[0] + skip * drive
            return states

        lax.fori_loop(0, span, advance, states, unroll=8)

    owned = (y * Z + z) * 4
    pick = lax.broadcasted_iota(jnp.int32, (8, width), 1) == lax.broadcasted_iota(jnp.int32, (8, width), 0) + owned
    pick = pick.astype(jnp.float32)
    contract = (((1,), (1,)), ((), ()))
    state = lax.dot_general(pick, last, contract, precision=EXACT, preferred_element_type=jnp.float32)
    flipped = lax.dot_general(last, pick, contract, precision=EXACT, preferred_element_type=jnp.float32)
    top = jnp.maximum(jnp.max(jnp.abs(state), axis=1, keepdims=True), 1.0)
    unit_ref[...] = (state / top)[:4]
    scale_ref[...] = (jnp.maximum(jnp.max(jnp.abs(flipped), axis=0, keepdims=True), 1.0) / 127.0)[:, :4]


def mix_kernel(features_ref, weights_ref, conv_ref, mixed_ref, total, *scratch):
    project(features_ref, weights_ref, *scratch[:2], total, *scratch[2:])
    query = total[0].astype(jnp.bfloat16).astype(jnp.float32)
    for half in range(conv_ref.shape[0]):
        here = slice(half * LANES, half * LANES + LANES)
        mixed_ref[:, here] = (query[:, here] * conv_ref[half]).astype(jnp.bfloat16)


def vmem():
    return pl.BlockSpec(memory_space=pltpu.VMEM)


def in_hbm(array):
    return pltpu.with_memory_space_constraint(array, pltpu.HBM)


def smem():
    return pl.BlockSpec(memory_space=pltpu.SMEM)


def shards(tokens, in_weight, rate, residue, skip_gain):
    rows, depth = tokens.shape
    width, poles = rate.shape
    y, z, x, k = (lax.axis_index(a) for a in AXES)
    f32 = functools.partial(jax.ShapeDtypeStruct, dtype=jnp.float32)
    bf16 = functools.partial(jax.ShapeDtypeStruct, dtype=jnp.bfloat16)

    def near_line(array):
        copies = jnp.broadcast_to(array[None], (LINE,) + array.shape)
        return lax.all_to_all(copies, AXES, 0, 0, tiled=True, axis_index_groups=lines(True))

    def far_line(array):
        return lax.all_gather(array, AXES, axis=0, axis_index_groups=lines(False))

    near_weights = near_line(in_weight.transpose(1, 0, 2))
    drive_weights = far_line(near_weights[:, 1:])

    blocks = tokens.reshape(rows, LINE, LANES).transpose(1, 0, 2) + near_weights[0, 0, 0, 0] * 0
    other = shifted(blocks, "k", 1)
    across = [shifted(blocks[: LINE // 2], "x", 2), shifted(blocks[LINE // 2 :], "x", -2)]
    arrived = [shifted(blocks, "x", 1), shifted(blocks, "x", -1)] + across
    remote = jnp.concatenate(arrived)
    pieces = [blocks, other, remote, shifted(remote, "k", 1)]
    chan = [2 * x + k, 2 * x + 1 - k] + [2 * ((x + d) % X) + e for e in (k, 1 - k) for d in (X - 1, 1, 2)]
    meta = jnp.stack(chan + [k, y, z]).astype(jnp.int32)
    features = pl.pallas_call(
        collect_kernel,
        in_specs=[smem()] + [vmem()] * 4,
        out_specs=vmem(),
        out_shape=bf16((LINE,) + blocks.shape),
        compiler_params=pltpu.CompilerParams(vmem_limit_bytes=16 * 2**20),
        name="collect",
    )(meta, *pieces)

    query_weights = far_line(near_weights[:, :1])

    def project_scratch(gathered):
        return [
            pltpu.VMEM((gathered.shape[2], rows, width), jnp.float32),
            pltpu.VMEM(features.shape, jnp.bfloat16),
            pltpu.VMEM(gathered.shape, jnp.bfloat16),
            pltpu.SemaphoreType.DMA((LINE,)),
            pltpu.SemaphoreType.DMA((LINE,)),
        ]

    rate_rows = rate.T
    filters = jnp.concatenate([rate_rows, residue.T, skip_gain[None]])
    params = pltpu.CompilerParams(vmem_limit_bytes=20 * 2**20)
    hbm = pl.BlockSpec(memory_space=pltpu.HBM)
    drive_shape = (width // LANES, rows, LANES)
    local_shape = (width // LANES, rows + poles * SUB, LANES)
    local, own = pl.pallas_call(
        drive_kernel,
        in_specs=[hbm, hbm, vmem()],
        out_specs=[vmem()] * 2,
        out_shape=[f32(local_shape), f32((poles, width))],
        scratch_shapes=[pltpu.VMEM((width // LANES, poles * SUB, LANES), jnp.float32)] + project_scratch(drive_weights),
        compiler_params=params,
        name="drive",
    )(in_hbm(features), in_hbm(drive_weights), filters)

    near = to_all(own, "z")
    at = jnp.arange(Z, dtype=jnp.float32)[:, None, None]
    gap = z.astype(jnp.float32) - 1.0 - at
    row_rate = rate_rows[None] * rows
    rows_in = jnp.sum(jnp.where(gap >= 0, jnp.exp(-row_rate * jnp.maximum(gap, 0.0)), 0.0) * near, axis=0)
    row_sum = jnp.sum(jnp.exp(-row_rate * (Z - 1.0 - at)) * near, axis=0)
    far = to_all(row_sum, "y")

    conv, unit, scale = pl.pallas_call(
        convolve_kernel,
        in_specs=[smem()] + [vmem()] * 4,
        out_specs=[vmem()] * 3,
        out_shape=[f32(drive_shape), f32((4, poles)), f32((1, 4))],
        compiler_params=params,
        name="convolve",
    )(meta, local, rows_in, far, filters)
    mixed = pl.pallas_call(
        mix_kernel,
        in_specs=[hbm, hbm, vmem()],
        out_specs=vmem(),
        out_shape=bf16((rows, width)),
        scratch_shapes=project_scratch(query_weights),
        compiler_params=params,
        name="mix",
    )(in_hbm(features), in_hbm(query_weights), conv)
    return mixed, unit, scale.reshape(4)


def solution(mesh):
    fine = Mesh(mesh.devices.reshape(Y, Z, X, K), AXES)
    seq, chan = ("y", "z"), ("x", "k")
    in_specs = (P(seq, chan), P(seq, None, chan), P(chan, None), P(chan, None), P(chan))
    out_specs = (P(seq, chan), P(chan + seq, None), P(chan + seq))
    return jax.shard_map(shards, mesh=fine, in_specs=in_specs, out_specs=out_specs, check_vma=False)
```

```python
import functools

import jax
import jax.numpy as jnp
from jax import lax
from jax.experimental import pallas as pl
from jax.experimental.pallas import tpu as pltpu
from jax.sharding import Mesh
from jax.sharding import PartitionSpec as P

Y, Z, X, K = 8, 8, 4, 2
LINE = 8
AXES = ("y", "z", "x", "k")
SUB = 8
LANES = 128
EARLY, LATE = (0, 1, -1, 2, -2, 3, -3), (4,)
EXACT = lax.Precision.HIGHEST


def number(y, z, x, k):
    return ((y * Z + z) * X + x) * K + k


def lines(first):
    groups = []
    for k in range(K):
        along_z = (k == 0) == first
        for x in range(X):
            for o in range(LINE):
                groups.append([number(o, i, x, k) if along_z else number(i, o, x, k) for i in range(LINE)])
    return groups


def shifted(array, axis, step):
    size = lax.axis_size(axis)
    return lax.ppermute(array, axis, [(i, (i + step) % size) for i in range(size)])


def to_all(array, axis):
    copies = jnp.broadcast_to(array[None], (lax.psum(1, axis),) + array.shape)
    return lax.all_to_all(copies, axis, 0, 0, tiled=True)


def turned(array, step):
    pairs = [(g[i], g[(i + step) % LINE]) for g in lines(False) for i in range(LINE)]
    return lax.ppermute(array, AXES, pairs)


def collect_kernel(meta_ref, pieces_ref, features_ref, tokens, sems):
    k = meta_ref[0]
    copies = [pltpu.make_async_copy(pieces_ref.at[piece], tokens.at[piece], sems.at[piece]) for piece in range(X * K)]
    for copy in copies:
        copy.start()
    for piece, copy in enumerate(copies):
        copy.wait()
        for block in range(LINE):
            chunk, part = jnp.where(k == 0, piece, block), jnp.where(k == 0, block, piece)
            features_ref[chunk, part] = tokens[piece, :, block * LANES : (block + 1) * LANES]


def multiply(steps, first, meta_ref, features_ref, weight_refs, total, weights, sems):
    streams, _, width = total.shape
    copies = []
    for i in range(len(steps)):
        halves = [ref.at[:, first : first + streams] for ref in (weight_refs[i], weight_refs[len(steps) + i])]
        copies.append([pltpu.make_async_copy(half, weights.at[i, j], sems.at[j, i]) for j, half in enumerate(halves)])
    for group in copies:
        for copy in group:
            copy.start()
    for i, step in enumerate(steps):
        chunk = lax.rem(meta_ref[1] - step + LINE, LINE)
        rows = jnp.concatenate([features_ref[chunk, part] for part in range(LINE)], axis=1)
        for copy in copies[i]:
            copy.wait()
        for stream in range(streams):
            block = weights[i, :, :, stream].reshape(-1, width)
            total[stream] += jnp.dot(rows, block, preferred_element_type=jnp.float32)


def begin_kernel(meta_ref, features_ref, *refs):
    count = 2 * len(EARLY)
    total_ref = refs[count]
    total_ref[...] = jnp.zeros_like(total_ref)
    multiply(EARLY, 1, meta_ref, features_ref, refs[:count], total_ref, *refs[count + 1 :])


def query_kernel(meta_ref, features_ref, *refs):
    steps = EARLY + LATE
    count = 2 * len(steps)
    query_ref, total = refs[count : count + 2]
    total[...] = jnp.zeros_like(total)
    multiply(steps, 0, meta_ref, features_ref, refs[:count], total, *refs[count + 2 :])
    query_ref[...] = total[0].astype(jnp.bfloat16)


def drive_kernel(meta_ref, features_ref, *refs):
    count = 2 * len(LATE)
    total_ref, filter_ref, local_ref, own_ref, ends, total = refs[count : count + 6]
    poles, width = own_ref.shape
    halves, rows = width // LANES, total.shape[1]
    span = rows // SUB
    total[...] = total_ref[...]
    multiply(LATE, 1, meta_ref, features_ref, refs[:count], total, *refs[count + 6 :])
    key, value = (total[stream].astype(jnp.bfloat16).astype(jnp.float32) for stream in range(2))
    for half in range(halves):
        here = slice(half * LANES, half * LANES + LANES)
        local_ref[half, :rows] = key[:, here] * value[:, here]
    for half in range(halves):
        here = slice(half * LANES, half * LANES + LANES)
        keep = [jnp.broadcast_to(jnp.exp(-filter_ref[n : n + 1, here]), (SUB, LANES)) for n in range(poles)]

        def advance(i, states):
            drive = local_ref[half, pl.ds(i, SUB, stride=span), :]
            return [s * a + drive for s, a in zip(states, keep)]

        states = lax.fori_loop(0, span, advance, [jnp.zeros((SUB, LANES), jnp.float32)] * poles, unroll=8)
        for n in range(poles):
            ends[half, n * SUB : (n + 1) * SUB, :] = states[n]
        across = jnp.exp(-filter_ref[:poles, here] * span)
        before = jnp.zeros((poles, LANES), jnp.float32)
        for b in range(SUB):
            local_ref[half, pl.ds(rows + b, poles, stride=SUB), :] = before
            before = before * across + ends[half, pl.ds(b, poles, stride=SUB), :]
        own_ref[:, here] = before


def finish_kernel(meta_ref, query_ref, local_ref, rows_in_ref, far_ref, filter_ref, mixed_ref, unit_ref, scale_ref, conv):
    halves, rows, _ = conv.shape
    poles, width = rows_in_ref.shape
    span = rows // SUB
    y, z = meta_ref[2], meta_ref[3]
    rate = filter_ref[:poles]
    incoming = jnp.zeros_like(rate)
    last = jnp.zeros_like(rate)
    hop = jnp.exp(-rate * (rows * Z))
    for other in range(Y):
        incoming = jnp.where(other < y, incoming * hop + far_ref[other], incoming)
        last = last * hop + far_ref[other]
    incoming = rows_in_ref[...] + incoming * jnp.exp(-rate * (rows * z).astype(jnp.float32))

    block = lax.broadcasted_iota(jnp.int32, (SUB, LANES), 0).astype(jnp.float32) * span
    for half in range(halves):
        here = slice(half * LANES, half * LANES + LANES)
        keep = [jnp.broadcast_to(jnp.exp(-rate[n : n + 1, here]), (SUB, LANES)) for n in range(poles)]
        gain = [jnp.broadcast_to(filter_ref[poles + n : poles + n + 1, here], (SUB, LANES)) for n in range(poles)]
        skip = jnp.broadcast_to(filter_ref[2 * poles : 2 * poles + 1, here], (SUB, LANES))
        states = [
            local_ref[half, rows + n * SUB : rows + (n + 1) * SUB, :] + incoming[n : n + 1, here] * jnp.exp(-rate[n : n + 1, here] * block)
            for n in range(poles)
        ]

        def advance(i, states):
            drive = local_ref[half, pl.ds(i, SUB, stride=span), :]
            states = [s * a + drive for s, a in zip(states, keep)]
            terms = [s * g for s, g in zip(states, gain)]
            while len(terms) > 1:
                terms = [a + b for a, b in zip(terms[::2], terms[1::2])]
            conv[half, pl.ds(i, SUB, stride=span), :] = terms[0] + skip * drive
            return states

        lax.fori_loop(0, span, advance, states, unroll=8)

    query = query_ref[...].astype(jnp.float32)
    for half in range(halves):
        here = slice(half * LANES, half * LANES + LANES)
        mixed_ref[:, here] = (query[:, here] * conv[half]).astype(jnp.bfloat16)

    owned = (y * Z + z) * 4
    pick = lax.broadcasted_iota(jnp.int32, (8, width), 1) == lax.broadcasted_iota(jnp.int32, (8, width), 0) + owned
    pick = pick.astype(jnp.float32)
    contract = (((1,), (1,)), ((), ()))
    state = lax.dot_general(pick, last, contract, precision=EXACT, preferred_element_type=jnp.float32)
    flipped = lax.dot_general(last, pick, contract, precision=EXACT, preferred_element_type=jnp.float32)
    top = jnp.maximum(jnp.max(jnp.abs(state), axis=1, keepdims=True), 1.0)
    unit_ref[...] = (state / top)[:4]
    scale_ref[...] = (jnp.maximum(jnp.max(jnp.abs(flipped), axis=0, keepdims=True), 1.0) / 127.0)[:, :4]


def vmem():
    return pl.BlockSpec(memory_space=pltpu.VMEM)


def in_hbm(array):
    return pltpu.with_memory_space_constraint(array, pltpu.HBM)


def smem():
    return pl.BlockSpec(memory_space=pltpu.SMEM)


def shards(tokens, in_weight, rate, residue, skip_gain):
    rows, depth = tokens.shape
    width, poles = rate.shape
    y, z, x, k = (lax.axis_index(a) for a in AXES)
    f32 = functools.partial(jax.ShapeDtypeStruct, dtype=jnp.float32)
    bf16 = functools.partial(jax.ShapeDtypeStruct, dtype=jnp.bfloat16)

    weights = in_weight.transpose(1, 0, 2)
    copies = jnp.broadcast_to(weights[None], (LINE,) + weights.shape)
    near = lax.all_to_all(copies, AXES, 0, 0, tiled=True, axis_index_groups=lines(True))

    half = LINE // 2
    front, back = near[:half], near[half:]

    lefts, rights = {0: front}, {0: back}
    for sign in (1, -1):
        for line in (lefts, rights):
            for step in (1, 2, 3):
                line[sign * step] = turned(line[sign * (step - 1)], sign)
    lefts[4], rights[4] = turned(lefts[3], 1), turned(rights[-3], -1)

    pieces = to_all(tokens, ("x", "k"))
    meta = jnp.stack([k, jnp.where(k == 0, y, z), y, z]).astype(jnp.int32)
    filters = jnp.concatenate([rate.T, residue.T, skip_gain[None]])
    params = pltpu.CompilerParams(vmem_limit_bytes=20 * 2**20)
    hbm = pl.BlockSpec(memory_space=pltpu.HBM)
    features = pl.pallas_call(
        collect_kernel,
        in_specs=[smem(), hbm],
        out_specs=vmem(),
        out_shape=bf16((LINE, LINE, rows, LANES)),
        scratch_shapes=[pltpu.VMEM((X * K,) + tokens.shape, jnp.bfloat16), pltpu.SemaphoreType.DMA((X * K,))],
        compiler_params=params,
        name="collect",
    )(meta, in_hbm(pieces))

    def chunks(steps):
        return [in_hbm(line[step]) for line in (lefts, rights) for step in steps]

    def buffers(steps, streams):
        return [
            pltpu.VMEM((len(steps), 2, half, streams) + near.shape[2:], jnp.bfloat16),
            pltpu.SemaphoreType.DMA((2, len(steps))),
        ]

    total = pl.pallas_call(
        begin_kernel,
        in_specs=[smem(), vmem()] + [hbm] * (2 * len(EARLY)),
        out_specs=vmem(),
        out_shape=f32((2, rows, width)),
        scratch_shapes=buffers(EARLY, 2),
        compiler_params=params,
        name="begin",
    )(meta, features, *chunks(EARLY))
    local_shape = (width // LANES, rows + poles * SUB, LANES)
    local, own = pl.pallas_call(
        drive_kernel,
        in_specs=[smem(), vmem()] + [hbm] * (2 * len(LATE)) + [vmem()] * 2,
        out_specs=[vmem()] * 2,
        out_shape=[f32(local_shape), f32((poles, width))],
        scratch_shapes=[
            pltpu.VMEM((width // LANES, poles * SUB, LANES), jnp.float32),
            pltpu.VMEM((2, rows, width), jnp.float32),
        ]
        + buffers(LATE, 2),
        compiler_params=params,
        name="drive",
    )(meta, features, *chunks(LATE), total, filters)

    beside = to_all(own, "z")
    at = jnp.arange(Z, dtype=jnp.float32)[:, None, None]
    gap = z.astype(jnp.float32) - 1.0 - at
    row_rate = rate.T[None] * rows
    rows_in = jnp.sum(jnp.where(gap >= 0, jnp.exp(-row_rate * jnp.maximum(gap, 0.0)), 0.0) * beside, axis=0)
    row_sum = jnp.sum(jnp.exp(-row_rate * (Z - 1.0 - at)) * beside, axis=0)
    far = to_all(row_sum, "y")

    query = pl.pallas_call(
        query_kernel,
        in_specs=[smem(), vmem()] + [hbm] * (2 * len(EARLY + LATE)),
        out_specs=vmem(),
        out_shape=bf16((rows, width)),
        scratch_shapes=[pltpu.VMEM((1, rows, width), jnp.float32)] + buffers(EARLY + LATE, 1),
        compiler_params=params,
        name="query",
    )(meta, features, *chunks(EARLY + LATE))
    mixed, unit, scale = pl.pallas_call(
        finish_kernel,
        in_specs=[smem()] + [vmem()] * 5,
        out_specs=[vmem()] * 3,
        out_shape=[bf16((rows, width)), f32((4, poles)), f32((1, 4))],
        scratch_shapes=[pltpu.VMEM((width // LANES, rows, LANES), jnp.float32)],
        compiler_params=params,
        name="finish",
    )(meta, query, local, rows_in, far, filters)
    return mixed, unit, scale.reshape(4)


def solution(mesh):
    fine = Mesh(mesh.devices.reshape(Y, Z, X, K), AXES)
    seq, chan = ("y", "z"), ("x", "k")
    in_specs = (P(seq, chan), P(seq, None, chan), P(chan, None), P(chan, None), P(chan))
    out_specs = (P(seq, chan), P(chan + seq, None), P(chan + seq))
    return jax.shard_map(shards, mesh=fine, in_specs=in_specs, out_specs=out_specs, check_vma=False)
```

```python
import functools

import jax
import jax.numpy as jnp
from jax import lax
from jax.experimental import pallas as pl
from jax.experimental.pallas import tpu as pltpu
from jax.sharding import Mesh
from jax.sharding import PartitionSpec as P

Y, Z, X, K = 8, 8, 4, 2
LINE = 8
AXES = ("y", "z", "x", "k")
SUB = 8
LANES = 128
EARLY, LATE = (0, 1, -1, 2, -2, 3, -3), (4,)
EXACT = lax.Precision.HIGHEST


def number(y, z, x, k):
    return ((y * Z + z) * X + x) * K + k


def lines(first):
    groups = []
    for k in range(K):
        along_z = (k == 0) == first
        for x in range(X):
            for o in range(LINE):
                groups.append([number(o, i, x, k) if along_z else number(i, o, x, k) for i in range(LINE)])
    return groups


def shifted(array, axis, step):
    size = lax.axis_size(axis)
    return lax.ppermute(array, axis, [(i, (i + step) % size) for i in range(size)])


def to_all(array, axis):
    copies = jnp.broadcast_to(array[None], (lax.psum(1, axis),) + array.shape)
    return lax.all_to_all(copies, axis, 0, 0, tiled=True)


def turned(array, step):
    pairs = [(g[i], g[(i + step) % LINE]) for g in lines(False) for i in range(LINE)]
    return lax.ppermute(array, AXES, pairs)


def collect_kernel(meta_ref, pieces_ref, features_ref, tokens, sems):
    k = meta_ref[0]
    copies = [pltpu.make_async_copy(pieces_ref.at[piece], tokens.at[piece], sems.at[piece]) for piece in range(X * K)]
    for copy in copies:
        copy.start()
    for piece, copy in enumerate(copies):
        copy.wait()
        for block in range(LINE):
            chunk, part = jnp.where(k == 0, piece, block), jnp.where(k == 0, block, piece)
            features_ref[chunk, part] = tokens[piece, :, block * LANES : (block + 1) * LANES]


def multiply(steps, first, meta_ref, features_ref, weight_refs, total, weights, sems):
    streams, _, width = total.shape
    copies = []
    for i in range(len(steps)):
        halves = [ref.at[:, first : first + streams] for ref in (weight_refs[i], weight_refs[len(steps) + i])]
        copies.append([pltpu.make_async_copy(half, weights.at[i, j], sems.at[j, i]) for j, half in enumerate(halves)])
    for group in copies:
        for copy in group:
            copy.start()
    for i, step in enumerate(steps):
        chunk = lax.rem(meta_ref[1] - step + LINE, LINE)
        rows = jnp.concatenate([features_ref[chunk, part] for part in range(LINE)], axis=1)
        for copy in copies[i]:
            copy.wait()
        for stream in range(streams):
            block = weights[i, :, :, stream].reshape(-1, width)
            total[stream] += jnp.dot(rows, block, preferred_element_type=jnp.float32)


def begin_kernel(meta_ref, features_ref, *refs):
    count = 2 * len(EARLY)
    total_ref = refs[count]
    total_ref[...] = jnp.zeros_like(total_ref)
    multiply(EARLY, 1, meta_ref, features_ref, refs[:count], total_ref, *refs[count + 1 :])


def query_kernel(meta_ref, features_ref, *refs):
    steps = EARLY + LATE
    count = 2 * len(steps)
    query_ref, total = refs[count : count + 2]
    total[...] = jnp.zeros_like(total)
    multiply(steps, 0, meta_ref, features_ref, refs[:count], total, *refs[count + 2 :])
    query_ref[...] = total[0].astype(jnp.bfloat16)


def drive_kernel(meta_ref, features_ref, front_ref, back_ref, total_ref, filter_ref, local_ref, own_ref, ends):
    copies, poles, width = own_ref.shape
    halves, rows = width // LANES, total_ref.shape[1]
    span = rows // SUB
    chunk = lax.rem(meta_ref[1] + LINE // 2, LINE)
    left = jnp.concatenate([features_ref[chunk, part] for part in range(LINE)], axis=1)
    total = []
    for stream in range(2):
        block = jnp.concatenate([ref[:, 1 + stream].reshape(-1, width) for ref in (front_ref, back_ref)], axis=0)
        total.append(total_ref[stream] + jnp.dot(left, block, preferred_element_type=jnp.float32))
    key, value = (total[stream].astype(jnp.bfloat16).astype(jnp.float32) for stream in range(2))
    for half in range(halves):
        here = slice(half * LANES, half * LANES + LANES)
        local_ref[half, :rows] = key[:, here] * value[:, here]
    for half in range(halves):
        here = slice(half * LANES, half * LANES + LANES)
        keep = [jnp.broadcast_to(jnp.exp(-filter_ref[n : n + 1, here]), (SUB, LANES)) for n in range(poles)]

        def advance(i, states):
            drive = local_ref[half, pl.ds(i, SUB, stride=span), :]
            return [s * a + drive for s, a in zip(states, keep)]

        states = lax.fori_loop(0, span, advance, [jnp.zeros((SUB, LANES), jnp.float32)] * poles, unroll=8)
        for n in range(poles):
            ends[half, n * SUB : (n + 1) * SUB, :] = states[n]
        across = jnp.exp(-filter_ref[:poles, here] * span)
        before = jnp.zeros((poles, LANES), jnp.float32)
        for b in range(SUB):
            local_ref[half, pl.ds(rows + b, poles, stride=SUB), :] = before
            before = before * across + ends[half, pl.ds(b, poles, stride=SUB), :]
        for copy in range(copies):
            own_ref[copy, :, here] = before


def finish_kernel(meta_ref, query_ref, local_ref, rows_in_ref, far_ref, filter_ref, mixed_ref, unit_ref, scale_ref, conv):
    halves, rows, _ = conv.shape
    poles, width = rows_in_ref.shape
    span = rows // SUB
    y, z = meta_ref[2], meta_ref[3]
    rate = filter_ref[:poles]
    incoming = jnp.zeros_like(rate)
    last = jnp.zeros_like(rate)
    hop = jnp.exp(-rate * (rows * Z))
    for other in range(Y):
        row = far_ref[other]
        incoming = jnp.where(other < y, incoming * hop + row, incoming)
        last = last * hop + row
    incoming = rows_in_ref[...] + incoming * jnp.exp(-rate * (rows * z).astype(jnp.float32))

    block = lax.broadcasted_iota(jnp.int32, (SUB, LANES), 0).astype(jnp.float32) * span
    for half in range(halves):
        here = slice(half * LANES, half * LANES + LANES)
        keep = [jnp.broadcast_to(jnp.exp(-rate[n : n + 1, here]), (SUB, LANES)) for n in range(poles)]
        gain = [jnp.broadcast_to(filter_ref[poles + n : poles + n + 1, here], (SUB, LANES)) for n in range(poles)]
        skip = jnp.broadcast_to(filter_ref[2 * poles : 2 * poles + 1, here], (SUB, LANES))
        states = [
            local_ref[half, rows + n * SUB : rows + (n + 1) * SUB, :] + incoming[n : n + 1, here] * jnp.exp(-rate[n : n + 1, here] * block)
            for n in range(poles)
        ]

        def advance(i, states):
            drive = local_ref[half, pl.ds(i, SUB, stride=span), :]
            states = [s * a + drive for s, a in zip(states, keep)]
            terms = [s * g for s, g in zip(states, gain)]
            while len(terms) > 1:
                terms = [a + b for a, b in zip(terms[::2], terms[1::2])]
            conv[half, pl.ds(i, SUB, stride=span), :] = terms[0] + skip * drive
            return states

        lax.fori_loop(0, span, advance, states, unroll=8)

    query = query_ref[...].astype(jnp.float32)
    for half in range(halves):
        here = slice(half * LANES, half * LANES + LANES)
        mixed_ref[:, here] = (query[:, here] * conv[half]).astype(jnp.bfloat16)

    owned = (y * Z + z) * 4
    pick = lax.broadcasted_iota(jnp.int32, (8, width), 1) == lax.broadcasted_iota(jnp.int32, (8, width), 0) + owned
    pick = pick.astype(jnp.float32)
    contract = (((1,), (1,)), ((), ()))
    state = lax.dot_general(pick, last, contract, precision=EXACT, preferred_element_type=jnp.float32)
    flipped = lax.dot_general(last, pick, contract, precision=EXACT, preferred_element_type=jnp.float32)
    top = jnp.maximum(jnp.max(jnp.abs(state), axis=1, keepdims=True), 1.0)
    unit_ref[...] = (state / top)[:4]
    scale_ref[...] = (jnp.maximum(jnp.max(jnp.abs(flipped), axis=0, keepdims=True), 1.0) / 127.0)[:, :4]


def vmem():
    return pl.BlockSpec(memory_space=pltpu.VMEM)


def in_hbm(array):
    return pltpu.with_memory_space_constraint(array, pltpu.HBM)


def smem():
    return pl.BlockSpec(memory_space=pltpu.SMEM)


def shards(tokens, in_weight, rate, residue, skip_gain):
    rows, depth = tokens.shape
    width, poles = rate.shape
    y, z, x, k = (lax.axis_index(a) for a in AXES)
    f32 = functools.partial(jax.ShapeDtypeStruct, dtype=jnp.float32)
    bf16 = functools.partial(jax.ShapeDtypeStruct, dtype=jnp.bfloat16)

    weights = in_weight.transpose(1, 0, 2)
    copies = jnp.broadcast_to(weights[None], (LINE,) + weights.shape)
    near = lax.all_to_all(copies, AXES, 0, 0, tiled=True, axis_index_groups=lines(True))

    half = LINE // 2
    front, back = near[:half], near[half:]

    lefts, rights = {0: front}, {0: back}
    for sign in (1, -1):
        for line in (lefts, rights):
            for step in (1, 2, 3):
                line[sign * step] = turned(line[sign * (step - 1)], sign)
    lefts[4], rights[4] = turned(lefts[3], 1), turned(rights[-3], -1)

    pieces = to_all(tokens, ("x", "k"))
    meta = jnp.stack([k, jnp.where(k == 0, y, z), y, z]).astype(jnp.int32)
    filters = jnp.concatenate([rate.T, residue.T, skip_gain[None]])
    params = pltpu.CompilerParams(vmem_limit_bytes=20 * 2**20)
    hbm = pl.BlockSpec(memory_space=pltpu.HBM)
    features = pl.pallas_call(
        collect_kernel,
        in_specs=[smem(), hbm],
        out_specs=vmem(),
        out_shape=bf16((LINE, LINE, rows, LANES)),
        scratch_shapes=[pltpu.VMEM((X * K,) + tokens.shape, jnp.bfloat16), pltpu.SemaphoreType.DMA((X * K,))],
        compiler_params=params,
        name="collect",
    )(meta, in_hbm(pieces))

    def chunks(steps):
        return [line[step] if step in LATE else in_hbm(line[step]) for line in (lefts, rights) for step in steps]

    def buffers(steps, streams):
        return [
            pltpu.VMEM((len(steps), 2, half, streams) + near.shape[2:], jnp.bfloat16),
            pltpu.SemaphoreType.DMA((2, len(steps))),
        ]

    total = pl.pallas_call(
        begin_kernel,
        in_specs=[smem(), vmem()] + [hbm] * (2 * len(EARLY)),
        out_specs=vmem(),
        out_shape=f32((2, rows, width)),
        scratch_shapes=buffers(EARLY, 2),
        compiler_params=params,
        name="begin",
    )(meta, features, *chunks(EARLY))
    local_shape = (width // LANES, rows + poles * SUB, LANES)
    local, own = pl.pallas_call(
        drive_kernel,
        in_specs=[smem()] + [vmem()] * 5,
        out_specs=[vmem()] * 2,
        out_shape=[f32(local_shape), f32((Z, poles, width))],
        scratch_shapes=[pltpu.VMEM((width // LANES, poles * SUB, LANES), jnp.float32)],
        compiler_params=params,
        name="drive",
    )(meta, features, lefts[4], rights[4], total, filters)

    beside = lax.all_to_all(own, "z", 0, 0, tiled=True)
    at = jnp.arange(Z, dtype=jnp.float32)[:, None, None]
    gap = z.astype(jnp.float32) - 1.0 - at
    row_rate = rate.T[None] * rows
    rows_in = jnp.sum(jnp.where(gap >= 0, jnp.exp(-row_rate * jnp.maximum(gap, 0.0)), 0.0) * beside, axis=0)
    row_sum = jnp.sum(jnp.exp(-row_rate * (Z - 1.0 - at)) * beside, axis=0)
    far = to_all(row_sum, "y")

    query = pl.pallas_call(
        query_kernel,
        in_specs=[smem(), vmem()] + ([hbm] * len(EARLY) + [vmem()]) * 2,
        out_specs=vmem(),
        out_shape=bf16((rows, width)),
        scratch_shapes=[pltpu.VMEM((1, rows, width), jnp.float32)] + buffers(EARLY + LATE, 1),
        compiler_params=params,
        name="query",
    )(meta, features, *chunks(EARLY + LATE))
    mixed, unit, scale = pl.pallas_call(
        finish_kernel,
        in_specs=[smem()] + [vmem()] * 5,
        out_specs=[vmem()] * 3,
        out_shape=[bf16((rows, width)), f32((4, poles)), f32((1, 4))],
        scratch_shapes=[pltpu.VMEM((width // LANES, rows, LANES), jnp.float32)],
        compiler_params=params,
        name="finish",
    )(meta, query, local, rows_in, far, filters)
    return mixed, unit, scale.reshape(4)


def solution(mesh):
    fine = Mesh(mesh.devices.reshape(Y, Z, X, K), AXES)
    seq, chan = ("y", "z"), ("x", "k")
    in_specs = (P(seq, chan), P(seq, None, chan), P(chan, None), P(chan, None), P(chan))
    out_specs = (P(seq, chan), P(chan + seq, None), P(chan + seq))
    return jax.shard_map(shards, mesh=fine, in_specs=in_specs, out_specs=out_specs, check_vma=False)
```

```python
import functools

import jax
import jax.numpy as jnp
from jax import lax
from jax.experimental import pallas as pl
from jax.experimental.pallas import tpu as pltpu
from jax.sharding import Mesh
from jax.sharding import PartitionSpec as P

Y, Z, X, K = 8, 8, 4, 2
LINE = 8
AXES = ("y", "z", "x", "k")
SUB = 8
LANES = 128
EARLY, LATE = (0, 1, -1, 2, -2, 3, -3), (4,)
EXACT = lax.Precision.HIGHEST


def number(y, z, x, k):
    return ((y * Z + z) * X + x) * K + k


def lines(first):
    groups = []
    for k in range(K):
        along_z = (k == 0) == first
        for x in range(X):
            for o in range(LINE):
                groups.append([number(o, i, x, k) if along_z else number(i, o, x, k) for i in range(LINE)])
    return groups


def shifted(array, axis, step):
    size = lax.axis_size(axis)
    return lax.ppermute(array, axis, [(i, (i + step) % size) for i in range(size)])


def to_all(array, axis):
    copies = jnp.broadcast_to(array[None], (lax.psum(1, axis),) + array.shape)
    return lax.all_to_all(copies, axis, 0, 0, tiled=True)


def turned(array, step):
    pairs = [(g[i], g[(i + step) % LINE]) for g in lines(False) for i in range(LINE)]
    return lax.ppermute(array, AXES, pairs)


def copies_kernel(array_ref, copies_ref, held, load_sem, sems):
    load = pltpu.make_async_copy(array_ref, held, load_sem)
    load.start()
    load.wait()
    stores = [pltpu.make_async_copy(held, copies_ref.at[i], sems.at[i]) for i in range(copies_ref.shape[0])]
    for store in stores:
        store.start()
    for store in stores:
        store.wait()


def collect_kernel(meta_ref, pieces_ref, features_ref, tokens, sems):
    k = meta_ref[0]
    copies = [pltpu.make_async_copy(pieces_ref.at[piece], tokens.at[piece], sems.at[piece]) for piece in range(X * K)]
    for copy in copies:
        copy.start()
    for piece, copy in enumerate(copies):
        copy.wait()
        for block in range(LINE):
            chunk, part = jnp.where(k == 0, piece, block), jnp.where(k == 0, block, piece)
            features_ref[chunk, part] = tokens[piece, :, block * LANES : (block + 1) * LANES]


def multiply(steps, first, meta_ref, features_ref, weight_refs, total, weights, sems):
    streams, _, width = total.shape
    copies = []
    for i in range(len(steps)):
        halves = [ref.at[:, first : first + streams] for ref in (weight_refs[i], weight_refs[len(steps) + i])]
        copies.append([pltpu.make_async_copy(half, weights.at[i, j], sems.at[j, i]) for j, half in enumerate(halves)])
    for group in copies:
        for copy in group:
            copy.start()
    for i, step in enumerate(steps):
        chunk = lax.rem(meta_ref[1] - step + LINE, LINE)
        rows = jnp.concatenate([features_ref[chunk, part] for part in range(LINE)], axis=1)
        for copy in copies[i]:
            copy.wait()
        for stream in range(streams):
            block = weights[i, :, :, stream].reshape(-1, width)
            total[stream] += jnp.dot(rows, block, preferred_element_type=jnp.float32)


def begin_kernel(meta_ref, features_ref, *refs):
    count = 2 * len(EARLY)
    total_ref = refs[count]
    total_ref[...] = jnp.zeros_like(total_ref)
    multiply(EARLY, 1, meta_ref, features_ref, refs[:count], total_ref, *refs[count + 1 :])


def query_kernel(meta_ref, features_ref, *refs):
    steps = EARLY + LATE
    count = 2 * len(steps)
    query_ref, total = refs[count : count + 2]
    total[...] = jnp.zeros_like(total)
    multiply(steps, 0, meta_ref, features_ref, refs[:count], total, *refs[count + 2 :])
    query_ref[...] = total[0].astype(jnp.bfloat16)


def drive_kernel(meta_ref, features_ref, *refs):
    count = 2 * len(LATE)
    total_ref, filter_ref, local_ref, own_ref, ends, total = refs[count : count + 6]
    poles, width = own_ref.shape
    halves, rows = width // LANES, total.shape[1]
    span = rows // SUB
    total[...] = total_ref[...]
    multiply(LATE, 1, meta_ref, features_ref, refs[:count], total, *refs[count + 6 :])
    key, value = (total[stream].astype(jnp.bfloat16).astype(jnp.float32) for stream in range(2))
    for half in range(halves):
        here = slice(half * LANES, half * LANES + LANES)
        local_ref[half, :rows] = key[:, here] * value[:, here]
    for half in range(halves):
        here = slice(half * LANES, half * LANES + LANES)
        keep = [jnp.broadcast_to(jnp.exp(-filter_ref[n : n + 1, here]), (SUB, LANES)) for n in range(poles)]

        def advance(i, states):
            drive = local_ref[half, pl.ds(i, SUB, stride=span), :]
            return [s * a + drive for s, a in zip(states, keep)]

        states = lax.fori_loop(0, span, advance, [jnp.zeros((SUB, LANES), jnp.float32)] * poles, unroll=8)
        for n in range(poles):
            ends[half, n * SUB : (n + 1) * SUB, :] = states[n]
        across = jnp.exp(-filter_ref[:poles, here] * span)
        before = jnp.zeros((poles, LANES), jnp.float32)
        for b in range(SUB):
            local_ref[half, pl.ds(rows + b, poles, stride=SUB), :] = before
            before = before * across + ends[half, pl.ds(b, poles, stride=SUB), :]
        own_ref[:, here] = before


def finish_kernel(meta_ref, query_ref, local_ref, rows_in_ref, far_ref, filter_ref, mixed_ref, unit_ref, scale_ref, conv):
    halves, rows, _ = conv.shape
    poles, width = rows_in_ref.shape
    span = rows // SUB
    y, z = meta_ref[2], meta_ref[3]
    rate = filter_ref[:poles]
    incoming = jnp.zeros_like(rate)
    last = jnp.zeros_like(rate)
    hop = jnp.exp(-rate * (rows * Z))
    for other in range(Y):
        incoming = jnp.where(other < y, incoming * hop + far_ref[other], incoming)
        last = last * hop + far_ref[other]
    incoming = rows_in_ref[...] + incoming * jnp.exp(-rate * (rows * z).astype(jnp.float32))

    block = lax.broadcasted_iota(jnp.int32, (SUB, LANES), 0).astype(jnp.float32) * span
    for half in range(halves):
        here = slice(half * LANES, half * LANES + LANES)
        keep = [jnp.broadcast_to(jnp.exp(-rate[n : n + 1, here]), (SUB, LANES)) for n in range(poles)]
        gain = [jnp.broadcast_to(filter_ref[poles + n : poles + n + 1, here], (SUB, LANES)) for n in range(poles)]
        skip = jnp.broadcast_to(filter_ref[2 * poles : 2 * poles + 1, here], (SUB, LANES))
        states = [
            local_ref[half, rows + n * SUB : rows + (n + 1) * SUB, :] + incoming[n : n + 1, here] * jnp.exp(-rate[n : n + 1, here] * block)
            for n in range(poles)
        ]

        def advance(i, states):
            drive = local_ref[half, pl.ds(i, SUB, stride=span), :]
            states = [s * a + drive for s, a in zip(states, keep)]
            terms = [s * g for s, g in zip(states, gain)]
            while len(terms) > 1:
                terms = [a + b for a, b in zip(terms[::2], terms[1::2])]
            conv[half, pl.ds(i, SUB, stride=span), :] = terms[0] + skip * drive
            return states

        lax.fori_loop(0, span, advance, states, unroll=8)

    query = query_ref[...].astype(jnp.float32)
    for half in range(halves):
        here = slice(half * LANES, half * LANES + LANES)
        mixed_ref[:, here] = (query[:, here] * conv[half]).astype(jnp.bfloat16)

    owned = (y * Z + z) * 4
    pick = lax.broadcasted_iota(jnp.int32, (8, width), 1) == lax.broadcasted_iota(jnp.int32, (8, width), 0) + owned
    pick = pick.astype(jnp.float32)
    contract = (((1,), (1,)), ((), ()))
    state = lax.dot_general(pick, last, contract, precision=EXACT, preferred_element_type=jnp.float32)
    flipped = lax.dot_general(last, pick, contract, precision=EXACT, preferred_element_type=jnp.float32)
    top = jnp.maximum(jnp.max(jnp.abs(state), axis=1, keepdims=True), 1.0)
    unit_ref[...] = (state / top)[:4]
    scale_ref[...] = (jnp.maximum(jnp.max(jnp.abs(flipped), axis=0, keepdims=True), 1.0) / 127.0)[:, :4]


def vmem():
    return pl.BlockSpec(memory_space=pltpu.VMEM)


def in_hbm(array):
    return pltpu.with_memory_space_constraint(array, pltpu.HBM)


def smem():
    return pl.BlockSpec(memory_space=pltpu.SMEM)


def shards(tokens, in_weight, rate, residue, skip_gain):
    rows, depth = tokens.shape
    width, poles = rate.shape
    y, z, x, k = (lax.axis_index(a) for a in AXES)
    f32 = functools.partial(jax.ShapeDtypeStruct, dtype=jnp.float32)
    bf16 = functools.partial(jax.ShapeDtypeStruct, dtype=jnp.bfloat16)

    weights = in_weight.transpose(1, 0, 2)
    copies = jnp.broadcast_to(weights[None], (LINE,) + weights.shape)
    near = lax.all_to_all(copies, AXES, 0, 0, tiled=True, axis_index_groups=lines(True))

    half = LINE // 2
    front, back = near[:half], near[half:]

    lefts, rights = {0: front}, {0: back}
    for sign in (1, -1):
        for line in (lefts, rights):
            for step in (1, 2, 3):
                line[sign * step] = turned(line[sign * (step - 1)], sign)
    lefts[4], rights[4] = turned(lefts[3], 1), turned(rights[-3], -1)

    hbm = pl.BlockSpec(memory_space=pltpu.HBM)
    token_copies = pl.pallas_call(
        copies_kernel,
        in_specs=[hbm],
        out_specs=hbm,
        out_shape=bf16((X * K,) + tokens.shape),
        scratch_shapes=[
            pltpu.VMEM(tokens.shape, jnp.bfloat16),
            pltpu.SemaphoreType.DMA(()),
            pltpu.SemaphoreType.DMA((X * K,)),
        ],
        name="copies",
    )(tokens)
    pieces = lax.all_to_all(token_copies, ("x", "k"), 0, 0, tiled=True)
    meta = jnp.stack([k, jnp.where(k == 0, y, z), y, z]).astype(jnp.int32)
    filters = jnp.concatenate([rate.T, residue.T, skip_gain[None]])
    params = pltpu.CompilerParams(vmem_limit_bytes=20 * 2**20)
    hbm = pl.BlockSpec(memory_space=pltpu.HBM)
    features = pl.pallas_call(
        collect_kernel,
        in_specs=[smem(), hbm],
        out_specs=vmem(),
        out_shape=bf16((LINE, LINE, rows, LANES)),
        scratch_shapes=[pltpu.VMEM((X * K,) + tokens.shape, jnp.bfloat16), pltpu.SemaphoreType.DMA((X * K,))],
        compiler_params=params,
        name="collect",
    )(meta, in_hbm(pieces))

    def chunks(steps):
        return [in_hbm(line[step]) for line in (lefts, rights) for step in steps]

    def buffers(steps, streams):
        return [
            pltpu.VMEM((len(steps), 2, half, streams) + near.shape[2:], jnp.bfloat16),
            pltpu.SemaphoreType.DMA((2, len(steps))),
        ]

    total = pl.pallas_call(
        begin_kernel,
        in_specs=[smem(), vmem()] + [hbm] * (2 * len(EARLY)),
        out_specs=vmem(),
        out_shape=f32((2, rows, width)),
        scratch_shapes=buffers(EARLY, 2),
        compiler_params=params,
        name="begin",
    )(meta, features, *chunks(EARLY))
    local_shape = (width // LANES, rows + poles * SUB, LANES)
    local, own = pl.pallas_call(
        drive_kernel,
        in_specs=[smem(), vmem()] + [hbm] * (2 * len(LATE)) + [vmem()] * 2,
        out_specs=[vmem()] * 2,
        out_shape=[f32(local_shape), f32((poles, width))],
        scratch_shapes=[
            pltpu.VMEM((width // LANES, poles * SUB, LANES), jnp.float32),
            pltpu.VMEM((2, rows, width), jnp.float32),
        ]
        + buffers(LATE, 2),
        compiler_params=params,
        name="drive",
    )(meta, features, *chunks(LATE), total, filters)

    beside = to_all(own, "z")
    at = jnp.arange(Z, dtype=jnp.float32)[:, None, None]
    gap = z.astype(jnp.float32) - 1.0 - at
    row_rate = rate.T[None] * rows
    rows_in = jnp.sum(jnp.where(gap >= 0, jnp.exp(-row_rate * jnp.maximum(gap, 0.0)), 0.0) * beside, axis=0)
    row_sum = jnp.sum(jnp.exp(-row_rate * (Z - 1.0 - at)) * beside, axis=0)
    far = to_all(row_sum, "y")

    query = pl.pallas_call(
        query_kernel,
        in_specs=[smem(), vmem()] + [hbm] * (2 * len(EARLY + LATE)),
        out_specs=vmem(),
        out_shape=bf16((rows, width)),
        scratch_shapes=[pltpu.VMEM((1, rows, width), jnp.float32)] + buffers(EARLY + LATE, 1),
        compiler_params=params,
        name="query",
    )(meta, features, *chunks(EARLY + LATE))
    mixed, unit, scale = pl.pallas_call(
        finish_kernel,
        in_specs=[smem()] + [vmem()] * 5,
        out_specs=[vmem()] * 3,
        out_shape=[bf16((rows, width)), f32((4, poles)), f32((1, 4))],
        scratch_shapes=[pltpu.VMEM((width // LANES, rows, LANES), jnp.float32)],
        compiler_params=params,
        name="finish",
    )(meta, query, local, rows_in, far, filters)
    return mixed, unit, scale.reshape(4)


def solution(mesh):
    fine = Mesh(mesh.devices.reshape(Y, Z, X, K), AXES)
    seq, chan = ("y", "z"), ("x", "k")
    in_specs = (P(seq, chan), P(seq, None, chan), P(chan, None), P(chan, None), P(chan))
    out_specs = (P(seq, chan), P(chan + seq, None), P(chan + seq))
    return jax.shard_map(shards, mesh=fine, in_specs=in_specs, out_specs=out_specs, check_vma=False)
```

```python
import functools

import jax
import jax.numpy as jnp
from jax import lax
from jax.experimental import pallas as pl
from jax.experimental.pallas import tpu as pltpu
from jax.sharding import Mesh
from jax.sharding import PartitionSpec as P

Y, Z, X, K = 8, 8, 4, 2
LINE = 8
AXES = ("y", "z", "x", "k")
SUB = 8
LANES = 128
EARLY, LATE = (0, 1, -1, 2, -2, 3, -3), (4,)
EXACT = lax.Precision.HIGHEST


def number(y, z, x, k):
    return ((y * Z + z) * X + x) * K + k


def lines(first):
    groups = []
    for k in range(K):
        along_z = (k == 0) == first
        for x in range(X):
            for o in range(LINE):
                groups.append([number(o, i, x, k) if along_z else number(i, o, x, k) for i in range(LINE)])
    return groups


def shifted(array, axis, step):
    size = lax.axis_size(axis)
    return lax.ppermute(array, axis, [(i, (i + step) % size) for i in range(size)])


def to_all(array, axis):
    copies = jnp.broadcast_to(array[None], (lax.psum(1, axis),) + array.shape)
    return lax.all_to_all(copies, axis, 0, 0, tiled=True)


def turned(array, step):
    pairs = [(g[i], g[(i + step) % LINE]) for g in lines(False) for i in range(LINE)]
    return lax.ppermute(array, AXES, pairs)


def copies_kernel(array_ref, copies_ref, held, load_sem, sems):
    load = pltpu.make_async_copy(array_ref, held, load_sem)
    load.start()
    load.wait()
    stores = [pltpu.make_async_copy(held, copies_ref.at[i], sems.at[i]) for i in range(copies_ref.shape[0])]
    for store in stores:
        store.start()
    for store in stores:
        store.wait()


def collect_kernel(meta_ref, pieces_ref, features_ref, tokens, sems):
    k = meta_ref[0]
    copies = [pltpu.make_async_copy(pieces_ref.at[piece], tokens.at[piece], sems.at[piece]) for piece in range(X * K)]
    for copy in copies:
        copy.start()
    for piece, copy in enumerate(copies):
        copy.wait()
        for block in range(LINE):
            chunk, part = jnp.where(k == 0, piece, block), jnp.where(k == 0, block, piece)
            features_ref[chunk, part] = tokens[piece, :, block * LANES : (block + 1) * LANES]


def multiply(steps, first, meta_ref, features_ref, weight_refs, total, weights, sems):
    streams, _, width = total.shape
    copies = []
    for i in range(len(steps)):
        halves = [ref.at[:, first : first + streams] for ref in (weight_refs[i], weight_refs[len(steps) + i])]
        copies.append([pltpu.make_async_copy(half, weights.at[i, j], sems.at[j, i]) for j, half in enumerate(halves)])
    for group in copies:
        for copy in group:
            copy.start()
    for i, step in enumerate(steps):
        chunk = lax.rem(meta_ref[1] - step + LINE, LINE)
        rows = jnp.concatenate([features_ref[chunk, part] for part in range(LINE)], axis=1)
        for copy in copies[i]:
            copy.wait()
        for stream in range(streams):
            block = weights[i, :, :, stream].reshape(-1, width)
            total[stream] += jnp.dot(rows, block, preferred_element_type=jnp.float32)


def begin_kernel(meta_ref, features_ref, *refs):
    count = 2 * len(EARLY)
    total_ref = refs[count]
    total_ref[...] = jnp.zeros_like(total_ref)
    multiply(EARLY, 1, meta_ref, features_ref, refs[:count], total_ref, *refs[count + 1 :])


def query_kernel(meta_ref, features_ref, *refs):
    steps = EARLY + LATE
    count = 2 * len(steps)
    query_ref, total = refs[count : count + 2]
    total[...] = jnp.zeros_like(total)
    multiply(steps, 0, meta_ref, features_ref, refs[:count], total, *refs[count + 2 :])
    query_ref[...] = total[0].astype(jnp.bfloat16)


def drive_kernel(meta_ref, features_ref, *refs):
    count = 2 * len(LATE)
    total_ref, filter_ref, local_ref, own_ref, ends, total = refs[count : count + 6]
    poles, width = own_ref.shape
    halves, rows = width // LANES, total.shape[1]
    span = rows // SUB
    total[...] = total_ref[...]
    multiply(LATE, 1, meta_ref, features_ref, refs[:count], total, *refs[count + 6 :])
    key, value = (total[stream].astype(jnp.bfloat16).astype(jnp.float32) for stream in range(2))
    for half in range(halves):
        here = slice(half * LANES, half * LANES + LANES)
        local_ref[half, :rows] = key[:, here] * value[:, here]
    for half in range(halves):
        here = slice(half * LANES, half * LANES + LANES)
        keep = [jnp.broadcast_to(jnp.exp(-filter_ref[n : n + 1, here]), (SUB, LANES)) for n in range(poles)]

        def advance(i, states):
            drive = local_ref[half, pl.ds(i, SUB, stride=span), :]
            return [s * a + drive for s, a in zip(states, keep)]

        states = lax.fori_loop(0, span, advance, [jnp.zeros((SUB, LANES), jnp.float32)] * poles, unroll=8)
        for n in range(poles):
            ends[half, n * SUB : (n + 1) * SUB, :] = states[n]
        across = jnp.exp(-filter_ref[:poles, here] * span)
        before = jnp.zeros((poles, LANES), jnp.float32)
        for b in range(SUB):
            local_ref[half, pl.ds(rows + b, poles, stride=SUB), :] = before
            before = before * across + ends[half, pl.ds(b, poles, stride=SUB), :]
        own_ref[:, here] = before


def finish_kernel(meta_ref, query_ref, local_ref, rows_in_ref, far_ref, filter_ref, mixed_ref, unit_ref, scale_ref, conv):
    halves, rows, _ = conv.shape
    poles, width = rows_in_ref.shape
    span = rows // SUB
    y, z = meta_ref[2], meta_ref[3]
    rate = filter_ref[:poles]
    incoming = jnp.zeros_like(rate)
    last = jnp.zeros_like(rate)
    hop = jnp.exp(-rate * (rows * Z))
    for other in range(Y):
        incoming = jnp.where(other < y, incoming * hop + far_ref[other], incoming)
        last = last * hop + far_ref[other]
    incoming = rows_in_ref[...] + incoming * jnp.exp(-rate * (rows * z).astype(jnp.float32))

    block = lax.broadcasted_iota(jnp.int32, (SUB, LANES), 0).astype(jnp.float32) * span
    for half in range(halves):
        here = slice(half * LANES, half * LANES + LANES)
        keep = [jnp.broadcast_to(jnp.exp(-rate[n : n + 1, here]), (SUB, LANES)) for n in range(poles)]
        gain = [jnp.broadcast_to(filter_ref[poles + n : poles + n + 1, here], (SUB, LANES)) for n in range(poles)]
        skip = jnp.broadcast_to(filter_ref[2 * poles : 2 * poles + 1, here], (SUB, LANES))
        states = [
            local_ref[half, rows + n * SUB : rows + (n + 1) * SUB, :] + incoming[n : n + 1, here] * jnp.exp(-rate[n : n + 1, here] * block)
            for n in range(poles)
        ]

        def advance(i, states):
            drive = local_ref[half, pl.ds(i, SUB, stride=span), :]
            states = [s * a + drive for s, a in zip(states, keep)]
            terms = [s * g for s, g in zip(states, gain)]
            while len(terms) > 1:
                terms = [a + b for a, b in zip(terms[::2], terms[1::2])]
            conv[half, pl.ds(i, SUB, stride=span), :] = terms[0] + skip * drive
            return states

        lax.fori_loop(0, span, advance, states, unroll=8)

    query = query_ref[...].astype(jnp.float32)
    for half in range(halves):
        here = slice(half * LANES, half * LANES + LANES)
        mixed_ref[:, here] = (query[:, here] * conv[half]).astype(jnp.bfloat16)

    owned = (y * Z + z) * 4
    pick = lax.broadcasted_iota(jnp.int32, (8, width), 1) == lax.broadcasted_iota(jnp.int32, (8, width), 0) + owned
    pick = pick.astype(jnp.float32)
    contract = (((1,), (1,)), ((), ()))
    state = lax.dot_general(pick, last, contract, precision=EXACT, preferred_element_type=jnp.float32)
    flipped = lax.dot_general(last, pick, contract, precision=EXACT, preferred_element_type=jnp.float32)
    top = jnp.maximum(jnp.max(jnp.abs(state), axis=1, keepdims=True), 1.0)
    unit_ref[...] = (state / top)[:4]
    scale_ref[...] = (jnp.maximum(jnp.max(jnp.abs(flipped), axis=0, keepdims=True), 1.0) / 127.0)[:, :4]


def vmem():
    return pl.BlockSpec(memory_space=pltpu.VMEM)


def in_hbm(array):
    return pltpu.with_memory_space_constraint(array, pltpu.HBM)


def smem():
    return pl.BlockSpec(memory_space=pltpu.SMEM)


def shards(tokens, in_weight, rate, residue, skip_gain):
    rows, depth = tokens.shape
    width, poles = rate.shape
    y, z, x, k = (lax.axis_index(a) for a in AXES)
    f32 = functools.partial(jax.ShapeDtypeStruct, dtype=jnp.float32)
    bf16 = functools.partial(jax.ShapeDtypeStruct, dtype=jnp.bfloat16)

    weights = in_weight.transpose(1, 0, 2)
    hbm = pl.BlockSpec(memory_space=pltpu.HBM)

    def eightfold(array):
        return pl.pallas_call(
            copies_kernel,
            in_specs=[hbm],
            out_specs=hbm,
            out_shape=bf16((LINE,) + array.shape),
            scratch_shapes=[
                pltpu.VMEM(array.shape, jnp.bfloat16),
                pltpu.SemaphoreType.DMA(()),
                pltpu.SemaphoreType.DMA((LINE,)),
            ],
            name="copies",
        )(array)

    copies = eightfold(weights)
    near = lax.all_to_all(copies, AXES, 0, 0, tiled=True, axis_index_groups=lines(True))

    half = LINE // 2
    front, back = near[:half], near[half:]

    lefts, rights = {0: front}, {0: back}
    for sign in (1, -1):
        for line in (lefts, rights):
            for step in (1, 2, 3):
                line[sign * step] = turned(line[sign * (step - 1)], sign)
    lefts[4], rights[4] = turned(lefts[3], 1), turned(rights[-3], -1)

    pieces = lax.all_to_all(eightfold(tokens), ("x", "k"), 0, 0, tiled=True)
    meta = jnp.stack([k, jnp.where(k == 0, y, z), y, z]).astype(jnp.int32)
    filters = jnp.concatenate([rate.T, residue.T, skip_gain[None]])
    params = pltpu.CompilerParams(vmem_limit_bytes=20 * 2**20)
    hbm = pl.BlockSpec(memory_space=pltpu.HBM)
    features = pl.pallas_call(
        collect_kernel,
        in_specs=[smem(), hbm],
        out_specs=vmem(),
        out_shape=bf16((LINE, LINE, rows, LANES)),
        scratch_shapes=[pltpu.VMEM((X * K,) + tokens.shape, jnp.bfloat16), pltpu.SemaphoreType.DMA((X * K,))],
        compiler_params=params,
        name="collect",
    )(meta, in_hbm(pieces))

    def chunks(steps):
        return [in_hbm(line[step]) for line in (lefts, rights) for step in steps]

    def buffers(steps, streams):
        return [
            pltpu.VMEM((len(steps), 2, half, streams) + near.shape[2:], jnp.bfloat16),
            pltpu.SemaphoreType.DMA((2, len(steps))),
        ]

    total = pl.pallas_call(
        begin_kernel,
        in_specs=[smem(), vmem()] + [hbm] * (2 * len(EARLY)),
        out_specs=vmem(),
        out_shape=f32((2, rows, width)),
        scratch_shapes=buffers(EARLY, 2),
        compiler_params=params,
        name="begin",
    )(meta, features, *chunks(EARLY))
    local_shape = (width // LANES, rows + poles * SUB, LANES)
    local, own = pl.pallas_call(
        drive_kernel,
        in_specs=[smem(), vmem()] + [hbm] * (2 * len(LATE)) + [vmem()] * 2,
        out_specs=[vmem()] * 2,
        out_shape=[f32(local_shape), f32((poles, width))],
        scratch_shapes=[
            pltpu.VMEM((width // LANES, poles * SUB, LANES), jnp.float32),
            pltpu.VMEM((2, rows, width), jnp.float32),
        ]
        + buffers(LATE, 2),
        compiler_params=params,
        name="drive",
    )(meta, features, *chunks(LATE), total, filters)

    beside = to_all(own, "z")
    at = jnp.arange(Z, dtype=jnp.float32)[:, None, None]
    gap = z.astype(jnp.float32) - 1.0 - at
    row_rate = rate.T[None] * rows
    rows_in = jnp.sum(jnp.where(gap >= 0, jnp.exp(-row_rate * jnp.maximum(gap, 0.0)), 0.0) * beside, axis=0)
    row_sum = jnp.sum(jnp.exp(-row_rate * (Z - 1.0 - at)) * beside, axis=0)
    far = to_all(row_sum, "y")

    query = pl.pallas_call(
        query_kernel,
        in_specs=[smem(), vmem()] + [hbm] * (2 * len(EARLY + LATE)),
        out_specs=vmem(),
        out_shape=bf16((rows, width)),
        scratch_shapes=[pltpu.VMEM((1, rows, width), jnp.float32)] + buffers(EARLY + LATE, 1),
        compiler_params=params,
        name="query",
    )(meta, features, *chunks(EARLY + LATE))
    mixed, unit, scale = pl.pallas_call(
        finish_kernel,
        in_specs=[smem()] + [vmem()] * 5,
        out_specs=[vmem()] * 3,
        out_shape=[bf16((rows, width)), f32((4, poles)), f32((1, 4))],
        scratch_shapes=[pltpu.VMEM((width // LANES, rows, LANES), jnp.float32)],
        compiler_params=params,
        name="finish",
    )(meta, query, local, rows_in, far, filters)
    return mixed, unit, scale.reshape(4)


def solution(mesh):
    fine = Mesh(mesh.devices.reshape(Y, Z, X, K), AXES)
    seq, chan = ("y", "z"), ("x", "k")
    in_specs = (P(seq, chan), P(seq, None, chan), P(chan, None), P(chan, None), P(chan))
    out_specs = (P(seq, chan), P(chan + seq, None), P(chan + seq))
    return jax.shard_map(shards, mesh=fine, in_specs=in_specs, out_specs=out_specs, check_vma=False)
```
